256 devices in a mesh: sec: 8 (over y, z_hi), row: 4 (over x), col: 8 (over z_lo, core).
Axes of the slice: x: 4, y: 4, z: 8 (z_hi: 2, z_lo: 4; z = z_hi * 4 + z_lo), core: 2. Of those that a mesh axis runs over, the one named last changes fastest.
Arguments:
- pairs: float32 [8, 2, 2048, 4096], P('sec', None, 'row', 'col'), may hold values from -0.75 to 0.75
Outputs:
- combined: float32 [8, 2, 2048, 4096], P('sec', None, 'row', 'col')
The draws below stay inside these ranges and needn't reach their ends.
All inputs are finite; a program needn't handle non-finite values.
Results may differ from the reference program's by a relative error of at most 0.0001.
Values sent between devices are 32-bit elements; how exact they have to be, the bound alone decides.
No kernel may reach another device: no remote copies, remote signals or barrier semaphores. Data moves between devices by JAX's collectives and lax.ppermute only.
A program may use at most 128 MiB of HBM per device.

```python
import jax
import jax.numpy as jnp
from jax import lax

M = 2048
GROUPS = 8
CB = 256
N_SEC = 8
N_COL = 8


def shard_levels(key, extent, shards, least, top_value):
    factor_of, own = 1.0, jax.random.fold_in(key, 6)
    for axis_at, shards_of in shards:
        steps = jnp.exp(jax.random.uniform(jax.random.fold_in(own, axis_at), (shards_of,), jnp.float32, least / len(shards), top_value / len(shards)))
        factor_of = factor_of * jnp.repeat(steps, extent[axis_at] // shards_of).reshape([-1 if axis == axis_at else 1 for axis in range(len(extent))])
    return factor_of


def scatter_about(stream_key, shape, width, bound, cuts=(), dtype=jnp.bfloat16):
    array = jax.random.normal(stream_key, shape, jnp.float32) * width
    if len(cuts) > 0:
        array = shard_levels(stream_key, shape, cuts, -0.22, 0.18) * array
    return jnp.clip(array, min=-bound, max=bound).astype(dtype)


def setup_inputs(seed: int = 0) -> dict:
    splits = jax.random.split(jax.random.key(seed), 2)
    pairs = scatter_about(splits[0], (GROUPS, 2, M, 2 * M), ((2 * M) ** -0.25), 0.75, ((0, 8), (2, 4), (3, 8)), jnp.float32)
    return dict(pairs=pairs)


def real_dot(left, right):
    return jnp.dot(left, right, precision=lax.Precision.HIGHEST, preferred_element_type=jnp.float32)


def complex_times(a_re, a_im, b_re, b_im):
    return real_dot(a_re, b_re) - real_dot(a_im, b_im), real_dot(a_re, b_im) + real_dot(a_im, b_re)


def unpack(packed):
    shaped = packed.reshape(2, M, N_COL, 2, CB)
    return jnp.transpose(shaped, (0, 3, 1, 2, 4)).reshape(2, 2, M, M)


def pack_up(parts):
    shaped = parts.reshape(2, 2, M, N_COL, CB)
    return jnp.transpose(shaped, (0, 2, 3, 1, 4)).reshape(2, M, 2 * M)


def reference(pairs):
    results = []
    for couple in range(N_SEC // 2):
        first_pair = unpack(pairs[2 * couple])
        second_pair = unpack(pairs[2 * couple + 1])
        prod_re, prod_im = complex_times(first_pair[0, 0], first_pair[0, 1], second_pair[0, 0], second_pair[0, 1])
        left_re, left_im = complex_times(first_pair[1, 0], first_pair[1, 1], second_pair[0, 0], second_pair[0, 1])
        right_re, right_im = complex_times(first_pair[0, 0], first_pair[0, 1], second_pair[1, 0], second_pair[1, 1])
        result = jnp.stack([jnp.stack([prod_re, prod_im]), jnp.stack([left_re + right_re, left_im + right_im])])
        packed = pack_up(result)
        results.append(packed)
        results.append(packed)
    return jnp.stack(results)
```

```python
import functools

import jax
import jax.numpy as jnp
from jax import lax
from jax.experimental import pallas as pl
from jax.experimental.pallas import tpu as pltpu
from jax.sharding import PartitionSpec as P

F32, BF16 = jnp.float32, jnp.bfloat16
N_Y, N_RING, N_CORE = 4, 8, 2
ROWS, BLOCK, HALF = 512, 512, 256

UP = [
    [(0, 1), (1, 2), (2, 3), (3, 4)],
    [(1, 2), (2, 3), (3, 4), (4, 5)],
    [(2, 3), (3, 4), (4, 5), (5, 6)],
    [(5, 6), (6, 7)],
]
DOWN = [[((3 - a) % 8, (3 - b) % 8) for a, b in step] for step in UP]
CROSS = [
    [(4, 6), (6, 0), (5, 3), (7, 5)],
    [(6, 0), (0, 2), (3, 1), (5, 3)],
]
EARLY = [
    [(0, 0), (5, 1), (6, 2)],
    [(0, 1), (1, 0), (5, 2)],
    [(0, 2), (1, 1), (5, 3)],
    [(0, 3), (1, 2), (2, 1)],
    [(1, 3), (2, 2), (3, 1)],
    [(2, 3), (3, 2), (7, 0)],
    [(3, 3), (6, 0), (7, 1)],
    [(5, 0), (6, 1), (7, 2)],
]
LATE = [
    [(7, 3)], [(6, 3)], [(2, 0)], [(3, 0)], [(8, 0)], [(8, 1)], [(4, 2)], [(4, 3)],
]


def ring_permute(x, pairs):
    full = [
        ((2 * y + a // 4) * 8 + (a % 4) * 2 + c, (2 * y + b // 4) * 8 + (b % 4) * 2 + c)
        for y in range(N_Y)
        for a, b in pairs
        for c in range(N_CORE)
    ]
    return lax.ppermute(x, ("sec", "col"), full)


def swap_cores(x):
    return lax.ppermute(x, "col", [(i, i ^ 1) for i in range(8)])


def split(x):
    hi = x.astype(BF16)
    return hi, (x - hi.astype(F32)).astype(BF16)


def product_kernel(slots, rows, n_bufs, n_second, add, table, *refs):
    bufs, refs = refs[:n_bufs], refs[n_bufs:]
    second, refs = refs[:n_second], refs[n_second:]
    if add:
        base, refs = refs[0], refs[1:]
    out, a_f32, b_f32, l_hi, l_lo, r_hi, r_lo, a_sem, b_sem = refs
    for s in range(slots):
        for b in range(n_bufs):
            @pl.when(table[2 * s] == b)
            def _():
                pltpu.make_async_copy(bufs[b], a_f32.at[s], a_sem.at[s]).start()
        k = table[2 * s + 1]
        for n in range(n_second):
            pltpu.make_async_copy(second[n].at[k], b_f32.at[n, s], b_sem.at[n, s]).start()
    for s in range(slots):
        at = pl.ds(s * HALF, HALF)
        pltpu.make_async_copy(bufs[0], a_f32.at[s], a_sem.at[s]).wait()
        for m in range(2):
            for p in range(2):
                hi, lo = split(a_f32[s, m, :, p * HALF:(p + 1) * HALF])
                l_hi[2 * m + p, :, at] = hi
                l_lo[2 * m + p, :, at] = lo
        for n in range(n_second):
            pltpu.make_async_copy(second[n].at[0], b_f32.at[n, s], b_sem.at[n, s]).wait()
            hi, lo = split(b_f32[n, s])
            r_hi[n, at, :] = hi
            r_lo[n, at, :] = lo
    depth = slots * HALF

    def dots(first, count, n):
        hi = l_hi[first:first + count].reshape(count * rows, depth)
        lo = l_lo[first:first + count].reshape(count * rows, depth)
        dot = functools.partial(jnp.dot, preferred_element_type=F32)
        return dot(hi, r_hi[n]) + dot(lo, r_hi[n]) + dot(hi, r_lo[n])

    def combine(x, y):
        return x[:, :HALF] - y[:, HALF:], x[:, HALF:] + y[:, :HALF]

    def store(m, side, re_im):
        for p in range(2):
            at = (m, slice(None), pl.ds(side * BLOCK + p * HALF, HALF))
            out[at] = re_im[p] + base[at] if add else re_im[p]

    for side in range(n_second // 2):
        both = dots(0, 4, 2 * side)
        store(0, side, combine(both[:rows], both[rows:2 * rows]))
        more = dots(0, 2, 2 * side + 1)
        store(1, side, combine(both[2 * rows:3 * rows] + more[:rows], both[3 * rows:] + more[rows:]))


def products(bufs, second, table, base=None):
    rows, slots = bufs[0].shape[1], table.shape[0] // 2
    n_second = len(second)
    width = n_second // 2 * BLOCK
    operands = [*bufs, *second] + ([] if base is None else [base])
    flops = 2 * 3 * 3 * rows * slots * BLOCK * width
    return pl.pallas_call(
        functools.partial(product_kernel, slots, rows, len(bufs), n_second, base is not None),
        out_shape=jax.ShapeDtypeStruct((2, rows, width), F32),
        grid_spec=pltpu.PrefetchScalarGridSpec(
            num_scalar_prefetch=1,
            grid=(),
            in_specs=[pl.BlockSpec(memory_space=pl.ANY)] * (len(bufs) + n_second)
            + ([] if base is None else [pl.BlockSpec(memory_space=pltpu.VMEM)]),
            out_specs=pl.BlockSpec(memory_space=pltpu.VMEM),
            scratch_shapes=[
                pltpu.VMEM((slots, 2, rows, BLOCK), F32),
                pltpu.VMEM((n_second, slots, HALF, BLOCK), F32),
                pltpu.VMEM((4, rows, slots * HALF), BF16),
                pltpu.VMEM((4, rows, slots * HALF), BF16),
                pltpu.VMEM((n_second, slots * HALF, BLOCK), BF16),
                pltpu.VMEM((n_second, slots * HALF, BLOCK), BF16),
                pltpu.SemaphoreType.DMA((slots,)),
                pltpu.SemaphoreType.DMA((n_second, slots)),
            ],
        ),
        compiler_params=pltpu.CompilerParams(vmem_limit_bytes=44 * 2**20),
        cost_estimate=pl.CostEstimate(flops=flops, bytes_accessed=8 * 2**20, transcendentals=0),
    )(table, *operands)


def shards(pairs):
    own = pairs[0]
    sec, col = lax.axis_index("sec"), lax.axis_index("col")
    upper, core = sec % 2, col % 2
    position = upper * 4 + col // 2

    pieces = [own[:, :HALF], own[:, HALF:]]
    rings = []
    for piece in pieces:
        bufs = {0: piece}
        up = down = piece
        for step in range(4):
            up, down = ring_permute(up, UP[step]), ring_permute(down, DOWN[step])
            bufs[1 + step], bufs[5 + step] = up, down
        rings.append([bufs[i] for i in range(9)])

    low, high = own[:, :HALF], own[:, HALF:]
    kept = jnp.where(core == 0, low, high)
    other = swap_cores(jnp.where(core == 0, high, low))
    second = []
    for mine in (other[0], other[1], kept[0], kept[1]):
        moved = ring_permute(ring_permute(mine, CROSS[0]), CROSS[1])
        second.append(lax.all_gather(jnp.where(upper == 1, mine, moved), "row"))

    early = jnp.array(EARLY, jnp.int32).reshape(8, 6)[position]
    late = jnp.array(LATE, jnp.int32).reshape(8, 2)[position]
    every = jnp.concatenate([early, late])
    first = products(rings[0], second, every)
    last = products(rings[1], second, late, products(rings[1], second, early))
    outs = [part[:, :, BLOCK:] + swap_cores(part[:, :, :BLOCK]) for part in (first, last)]
    return jnp.concatenate(outs, axis=1)[None]


def solution(mesh):
    placed = (P("sec", None, "row", "col"),)
    return jax.shard_map(
        shards, mesh=mesh, in_specs=placed, out_specs=P("sec", None, "row", "col"), check_vma=False
    )
```

```python
import functools

import jax
import jax.numpy as jnp
from jax import lax
from jax.experimental import pallas as pl
from jax.experimental.pallas import tpu as pltpu
from jax.sharding import PartitionSpec as P

F32, BF16 = jnp.float32, jnp.bfloat16
N_Y, N_RING, N_CORE = 4, 8, 2
ROWS, BLOCK, HALF = 512, 512, 256

UP = [
    [(0, 1), (1, 2), (2, 3), (3, 4)],
    [(2, 3), (3, 4), (4, 5)],
    [(3, 4), (4, 5), (5, 6)],
    [(5, 6), (6, 7)],
]
LAST = [[(1, 2), (2, 1)], [(2, 3), (1, 0)]]
CROSS = [[(4, 0), (7, 3)], [(5, 1), (6, 2)]]
EARLY = [
    [(0, 0), (5, 1), (6, 2)],
    [(0, 1), (1, 0), (5, 2)],
    [(0, 2), (1, 1), (5, 3)],
    [(0, 3), (1, 2), (2, 1)],
    [(1, 3), (2, 2), (3, 1)],
    [(2, 3), (3, 2), (7, 0)],
    [(3, 3), (6, 0), (7, 1)],
    [(5, 0), (6, 1), (7, 2)],
]
LATE = [[(10, 3)], [(9, 3)], [(9, 0)], [(10, 0)], [(8, 0)], [(8, 1)], [(4, 2)], [(4, 3)]]


def ring_permute(x, pairs):
    full = [
        ((2 * y + a // 4) * 8 + (a % 4) * 2 + c, (2 * y + b // 4) * 8 + (b % 4) * 2 + c)
        for y in range(N_Y)
        for a, b in pairs
        for c in range(N_CORE)
    ]
    return lax.ppermute(x, ("sec", "col"), full)


def mirrored(pairs):
    return [((3 - a) % 8, (3 - b) % 8) for a, b in pairs]


def swap_cores(x):
    return lax.ppermute(x, "col", [(i, i ^ 1) for i in range(8)])


def split(x):
    hi = x.astype(BF16)
    return hi, (x - hi.astype(F32)).astype(BF16)


def product_kernel(slots, rows, n_bufs, layout, add, table, *refs):
    bufs, refs = refs[:n_bufs], refs[n_bufs:]
    n_second = len(layout)
    second = []
    for parts in layout:
        second.append([ref if part is None else ref.at[part] for ref, part in zip(refs, parts)])
        refs = refs[len(parts):]
    if add:
        base, refs = refs[0], refs[1:]
    out, a_f32, b_f32, left, right, a_sem, b_sem = refs
    depth = slots * 3 * HALF
    for s in range(slots):
        for b in range(n_bufs):
            @pl.when(table[2 * s] == b)
            def _():
                pltpu.make_async_copy(bufs[b], a_f32.at[s], a_sem.at[s]).start()
        for n in range(n_second):
            for i in range(4):
                @pl.when(table[2 * s + 1] == i)
                def _():
                    pltpu.make_async_copy(second[n][i], b_f32.at[n, s], b_sem.at[n, s]).start()
    for s in range(slots):
        pltpu.make_async_copy(a_f32.at[s], a_f32.at[s], a_sem.at[s]).wait()
        for m in range(2):
            at = (1 - m) * depth + s * 3 * HALF
            for p in range(2):
                hi, lo = split(a_f32[s, m, :, p * HALF:(p + 1) * HALF])
                for i, part in enumerate((hi, lo, hi)):
                    left[p * rows:(p + 1) * rows, at + i * HALF:at + (i + 1) * HALF] = part
        for n in range(n_second):
            pltpu.make_async_copy(b_f32.at[n, s], b_f32.at[n, s], b_sem.at[n, s]).wait()
            at = n % 2 * depth + s * 3 * HALF
            hi, lo = split(b_f32[n, s])
            for i, part in enumerate((hi, hi, lo)):
                right[n // 2, at + i * HALF:at + (i + 1) * HALF, :] = part

    def combine(x, y):
        return x[:, :HALF] - y[:, HALF:], x[:, HALF:] + y[:, :HALF]

    def store(m, side, re_im):
        for p in range(2):
            at = (m, slice(None), pl.ds(side * BLOCK + p * HALF, HALF))
            out[at] = re_im[p] + base[at] if add else re_im[p]

    for side in range(n_second // 2):
        value = jnp.dot(left[:, depth:], right[side, :depth], preferred_element_type=F32)
        store(0, side, combine(value[:rows], value[rows:]))
        slope = jnp.dot(left[...], right[side], preferred_element_type=F32)
        store(1, side, combine(slope[:rows], slope[rows:]))


def products(bufs, second, table, base=None):
    rows, slots = bufs[0].shape[1], table.shape[0] // 2
    n_second = len(second)
    layout = [[part for _, part in members] for members in second]
    width = n_second // 2 * BLOCK
    operands = [*bufs, *[ref for members in second for ref, _ in members]]
    n_any = len(operands)
    operands += [] if base is None else [base]
    return pl.pallas_call(
        functools.partial(product_kernel, slots, rows, len(bufs), layout, base is not None),
        out_shape=jax.ShapeDtypeStruct((2, rows, width), F32),
        grid_spec=pltpu.PrefetchScalarGridSpec(
            num_scalar_prefetch=1,
            grid=(),
            in_specs=[pl.BlockSpec(memory_space=pl.ANY)] * n_any
            + ([] if base is None else [pl.BlockSpec(memory_space=pltpu.VMEM)]),
            out_specs=pl.BlockSpec(memory_space=pltpu.VMEM),
            scratch_shapes=[
                pltpu.VMEM((slots, 2, rows, BLOCK), F32),
                pltpu.VMEM((n_second, slots, HALF, BLOCK), F32),
                pltpu.VMEM((2 * rows, 6 * slots * HALF), BF16),
                pltpu.VMEM((n_second // 2, 6 * slots * HALF, BLOCK), BF16),
                pltpu.SemaphoreType.DMA((slots,)),
                pltpu.SemaphoreType.DMA((n_second, slots)),
            ],
        ),
        compiler_params=pltpu.CompilerParams(vmem_limit_bytes=62 * 2**20),
        cost_estimate=pl.CostEstimate(flops=1024, bytes_accessed=1024, transcendentals=0),
    )(table, *operands)


def after(x, *earlier):
    return lax.optimization_barrier((x, *earlier))[0]


def shards(pairs):
    own = pairs[0]
    sec, row, col = (lax.axis_index(name) for name in ("sec", "row", "col"))
    upper, core = sec % 2, col % 2
    position = upper * 4 + col // 2

    def across(x, by):
        return lax.ppermute(x, "row", [(i, (i + by) % 4) for i in range(4)])

    def both(x, pairs, *earlier):
        x = tuple(after(part, *earlier) if earlier else part for part in x)
        return ring_permute(x[0], pairs), ring_permute(x[1], mirrored(pairs))

    one = both((own, own), UP[0])
    crossed = ring_permute(own, CROSS[0])
    two = both(one, UP[1], *one, crossed)
    crossed_late = ring_permute(after(own, *one, crossed), CROSS[1])
    three = both(two, UP[2], *two, crossed_late)
    last = after(jnp.where(position == 1, *one), *two, crossed_late)
    last = ring_permute(last, LAST[0])
    inner = (position == 1) | (position == 2)
    mine = jnp.where(upper == 1, own, jnp.where(inner, after(crossed_late, *two), crossed))
    low, high = mine[:, :HALF], mine[:, HALF:]
    kept = jnp.where(core == 0, low, high)
    other = swap_cores(jnp.where(core == 0, high, low))
    near = jnp.stack([other, kept])
    right, left = across(near, 1), across(near, -1)
    four = both(three, UP[3], *three, right, left)
    very_last = ring_permute(after(last, *three, right, left), LAST[1])
    right, left = after(right, *three), after(left, *three)
    far = across(right[0], 1), across(left[1], -1)
    second = [
        [(near, (side, m)), (left, (side, m)), (far[side], m), (right, (side, m))]
        for side in range(2)
        for m in range(2)
    ]
    up, down = zip(one, two, three, four)
    ring = [own, *up, *down, last, very_last]

    def table_of(entries, slots):
        flat = jnp.array(entries, jnp.int32).reshape(8, slots, 2)[position]
        return jnp.stack([flat[:, 0], (flat[:, 1] - row) % 4], axis=1).reshape(-1)

    shifted = [[(b - (b > 4), k) for b, k in entry] for entry in EARLY]
    early, late = table_of(shifted, 3), table_of(LATE, 1)
    early_ring = [ring[i] for i in (0, 1, 2, 3, 5, 6, 7)]
    total = products(ring, second, late, products(early_ring, second, early))
    return (total[:, :, BLOCK:] + swap_cores(total[:, :, :BLOCK]))[None]


def solution(mesh):
    placed = (P("sec", None, "row", "col"),)
    return jax.shard_map(
        shards, mesh=mesh, in_specs=placed, out_specs=P("sec", None, "row", "col"), check_vma=False
    )
```

```python
import functools

import jax
import jax.numpy as jnp
from jax import lax
from jax.experimental import pallas as pl
from jax.experimental.pallas import tpu as pltpu
from jax.sharding import PartitionSpec as P

F32, BF16 = jnp.float32, jnp.bfloat16
N_Y, N_RING, N_CORE = 4, 8, 2
ROWS, BLOCK, HALF = 512, 512, 256

UP = [
    [(0, 1), (1, 2), (2, 3), (3, 4)],
    [(2, 3), (3, 4), (4, 5)],
    [(3, 4), (4, 5), (5, 6)],
    [(5, 6), (6, 7)],
]
LAST = [[(1, 2), (2, 1)], [(2, 3), (1, 0)]]
CROSS = [[(4, 0), (7, 3)], [(5, 1), (6, 2)]]
EARLY = [
    [(0, 0), (5, 1), (6, 2)],
    [(0, 1), (1, 0), (5, 2)],
    [(0, 2), (1, 1), (5, 3)],
    [(0, 3), (1, 2), (2, 1)],
    [(1, 3), (2, 2), (3, 1)],
    [(2, 3), (3, 2), (7, 0)],
    [(3, 3), (6, 0), (7, 1)],
    [(5, 0), (6, 1), (7, 2)],
]
LATE = [[(10, 3)], [(9, 3)], [(9, 0)], [(10, 0)], [(8, 0)], [(8, 1)], [(4, 2)], [(4, 3)]]


def ring_permute(x, pairs):
    full = [
        ((2 * y + a // 4) * 8 + (a % 4) * 2 + c, (2 * y + b // 4) * 8 + (b % 4) * 2 + c)
        for y in range(N_Y)
        for a, b in pairs
        for c in range(N_CORE)
    ]
    return lax.ppermute(x, ("sec", "col"), full)


def mirrored(pairs):
    return [((3 - a) % 8, (3 - b) % 8) for a, b in pairs]


def swap_cores(x):
    return lax.ppermute(x, "col", [(i, i ^ 1) for i in range(8)])


def split(x):
    hi = x.astype(BF16)
    return hi, (x - hi.astype(F32)).astype(BF16)


def product_kernel(slots, rows, n_bufs, layout, add, table, *refs):
    bufs, refs = refs[:n_bufs], refs[n_bufs:]
    n_second = len(layout)
    second = []
    for parts in layout:
        second.append([ref if part is None else ref.at[part] for ref, part in zip(refs, parts)])
        refs = refs[len(parts):]
    if add:
        base, refs = refs[:n_second // 2], refs[n_second // 2:]
    outs, refs = refs[:n_second // 2], refs[n_second // 2:]
    a_f32, b_f32, left, right, a_sem, b_sem = refs
    depth = slots * 3 * HALF
    for s in range(slots):
        for b in range(n_bufs):
            @pl.when(table[2 * s] == b)
            def _():
                pltpu.make_async_copy(bufs[b], a_f32.at[s], a_sem.at[s]).start()
        for n in range(n_second):
            for i in range(len(second[n])):
                @pl.when(table[2 * s + 1] == i)
                def _():
                    pltpu.make_async_copy(second[n][i], b_f32.at[n, s], b_sem.at[n, s]).start()
    for s in range(slots):
        pltpu.make_async_copy(a_f32.at[s], a_f32.at[s], a_sem.at[s]).wait()
        for m in range(2):
            at = (1 - m) * depth + s * 3 * HALF
            for p in range(2):
                hi, lo = split(a_f32[s, m, :, p * HALF:(p + 1) * HALF])
                for i, part in enumerate((hi, lo, hi)):
                    left[p * rows:(p + 1) * rows, at + i * HALF:at + (i + 1) * HALF] = part
        for n in range(n_second):
            pltpu.make_async_copy(b_f32.at[n, s], b_f32.at[n, s], b_sem.at[n, s]).wait()
            at = n % 2 * depth + s * 3 * HALF
            hi, lo = split(b_f32[n, s])
            for i, part in enumerate((hi, hi, lo)):
                right[n // 2, at + i * HALF:at + (i + 1) * HALF, :] = part

    def combine(x, y):
        return x[:, :HALF] - y[:, HALF:], x[:, HALF:] + y[:, :HALF]

    def store(m, side, re_im):
        for p in range(2):
            at = (m, slice(None), slice(p * HALF, (p + 1) * HALF))
            outs[side][at] = re_im[p] + base[side][at] if add else re_im[p]

    for side in range(n_second // 2):
        value = jnp.dot(left[:, depth:], right[side, :depth], preferred_element_type=F32)
        store(0, side, combine(value[:rows], value[rows:]))
        slope = jnp.dot(left[...], right[side], preferred_element_type=F32)
        store(1, side, combine(slope[:rows], slope[rows:]))


def products(bufs, second, table, base=None):
    rows, slots = bufs[0].shape[1], table.shape[0] // 2
    n_second = len(second)
    layout = [[part for _, part in members] for members in second]
    sides = n_second // 2
    operands = [*bufs, *[ref for members in second for ref, _ in members]]
    n_any = len(operands)
    operands += [] if base is None else base
    return pl.pallas_call(
        functools.partial(product_kernel, slots, rows, len(bufs), layout, base is not None),
        out_shape=[jax.ShapeDtypeStruct((2, rows, BLOCK), F32)] * sides,
        grid_spec=pltpu.PrefetchScalarGridSpec(
            num_scalar_prefetch=1,
            grid=(),
            in_specs=[pl.BlockSpec(memory_space=pl.ANY)] * n_any
            + [pl.BlockSpec(memory_space=pltpu.VMEM)] * (len(operands) - n_any),
            out_specs=[pl.BlockSpec(memory_space=pltpu.VMEM)] * sides,
            scratch_shapes=[
                pltpu.VMEM((slots, 2, rows, BLOCK), F32),
                pltpu.VMEM((n_second, slots, HALF, BLOCK), F32),
                pltpu.VMEM((2 * rows, 6 * slots * HALF), BF16),
                pltpu.VMEM((n_second // 2, 6 * slots * HALF, BLOCK), BF16),
                pltpu.SemaphoreType.DMA((slots,)),
                pltpu.SemaphoreType.DMA((n_second, slots)),
            ],
        ),
        compiler_params=pltpu.CompilerParams(vmem_limit_bytes=62 * 2**20),
        cost_estimate=pl.CostEstimate(flops=1024, bytes_accessed=1024, transcendentals=0),
    )(table, *operands)


def after(x, *earlier):
    return lax.optimization_barrier((x, *earlier))[0]


def shards(pairs):
    own = pairs[0]
    sec, row, col = (lax.axis_index(name) for name in ("sec", "row", "col"))
    upper, core = sec % 2, col % 2
    position = upper * 4 + col // 2

    def across(x, by):
        return lax.ppermute(x, "row", [(i, (i + by) % 4) for i in range(4)])

    def both(x, pairs, *earlier):
        x = tuple(after(part, *earlier) if earlier else part for part in x)
        return ring_permute(x[0], pairs), ring_permute(x[1], mirrored(pairs))

    one = both((own, own), UP[0])
    low, high = own[:, :HALF], own[:, HALF:]
    kept = jnp.where(core == 0, low, high)
    near = jnp.stack([swap_cores(jnp.where(core == 0, high, low)), kept])
    crossed = ring_permute(near, CROSS[0])
    two = both(one, UP[1], *one, crossed)
    crossed_late = ring_permute(after(near, *one, crossed), CROSS[1])
    three = both(two, UP[2], *two, crossed_late)
    last = after(jnp.where(position == 1, *one), *two, crossed_late)
    last = ring_permute(last, LAST[0])
    inner = (position == 1) | (position == 2)
    near = jnp.where(upper == 1, near, jnp.where(inner, after(crossed_late, *two), crossed))
    right, left = across(near, 1), across(near, -1)
    four = both(three, UP[3], *three, right, left)
    very_last = ring_permute(after(last, *three, right, left), LAST[1])
    right, left = after(right, *three), after(left, *three)
    far = across(right[0], 1), across(left[1], -1)
    second = [
        [(near, (side, m)), (left, (side, m)), (far[side], m), (right, (side, m))]
        for side in range(2)
        for m in range(2)
    ]
    up, down = zip(one, two, three, four)
    ring = [own, *up, *down, last, very_last]

    def table_of(slots, bufs, members):
        rows = [
            [
                [(bufs.index(b), members.index((k - r) % 4)) for b, k in slots(EARLY[p], LATE[p], r)]
                for r in range(4)
            ]
            for p in range(N_RING)
        ]
        return jnp.array(rows, jnp.int32).reshape(N_RING, 4, -1)[position, row]

    def ordered(early, r):
        return sorted(early, key=lambda slot: (slot[1] - r) % 4 == 2)

    early_bufs, late_bufs = (0, 1, 2, 3, 5, 6, 7), (4, 8, 9, 10)
    early_ring, late_ring = [ring[i] for i in early_bufs], [ring[i] for i in late_bufs]
    close = [[members[i] for i in (0, 1, 3)] for members in second]
    first = table_of(lambda early, late, r: ordered(early, r)[:2], early_bufs, (0, 1, 3))
    third = table_of(lambda early, late, r: ordered(early, r)[2:], early_bufs, (0, 1, 2, 3))
    final = table_of(lambda early, late, r: late, late_bufs, (0, 1, 2, 3))
    total = products(early_ring, close, first)
    total = products(early_ring, second, third, total)
    total = products(late_ring, second, final, total)
    return (total[1] + swap_cores(total[0]))[None]


def solution(mesh):
    placed = (P("sec", None, "row", "col"),)
    return jax.shard_map(
        shards, mesh=mesh, in_specs=placed, out_specs=P("sec", None, "row", "col"), check_vma=False
    )
```

```python
import functools

import jax
import jax.numpy as jnp
from jax import lax
from jax.experimental import pallas as pl
from jax.experimental.pallas import tpu as pltpu
from jax.sharding import PartitionSpec as P

F32, BF16 = jnp.float32, jnp.bfloat16
N_Y, N_RING, N_CORE = 4, 8, 2
ROWS, BLOCK, HALF = 512, 512, 256

UP = [
    [(0, 1), (1, 2), (2, 3), (3, 4)],
    [(2, 3), (3, 4), (4, 5)],
    [(3, 4), (4, 5), (5, 6)],
    [(5, 6), (6, 7)],
]
LAST = [[(1, 2), (2, 1)], [(2, 3), (1, 0)]]
CROSS = [[(4, 0), (7, 3)], [(5, 1), (6, 2)]]
EARLY = [
    [(0, 0), (5, 1), (6, 2)],
    [(0, 1), (1, 0), (5, 2)],
    [(0, 2), (1, 1), (5, 3)],
    [(0, 3), (1, 2), (2, 1)],
    [(1, 3), (2, 2), (3, 1)],
    [(2, 3), (3, 2), (7, 0)],
    [(3, 3), (6, 0), (7, 1)],
    [(5, 0), (6, 1), (7, 2)],
]
LATE = [[(10, 3)], [(9, 3)], [(9, 0)], [(10, 0)], [(8, 0)], [(8, 1)], [(4, 2)], [(4, 3)]]


def ring_permute(x, pairs):
    full = [
        ((2 * y + a // 4) * 8 + (a % 4) * 2 + c, (2 * y + b // 4) * 8 + (b % 4) * 2 + c)
        for y in range(N_Y)
        for a, b in pairs
        for c in range(N_CORE)
    ]
    return lax.ppermute(x, ("sec", "col"), full)


def mirrored(pairs):
    return [((3 - a) % 8, (3 - b) % 8) for a, b in pairs]


def swap_cores(x):
    return lax.ppermute(x, "col", [(i, i ^ 1) for i in range(8)])


def split(x):
    hi = x.astype(BF16)
    return hi, (x - hi.astype(F32)).astype(BF16)


def product_kernel(slots, rows, n_bufs, layout, add, table, *refs):
    bufs, refs = refs[:n_bufs], refs[n_bufs:]
    n_second = len(layout)
    second = []
    for parts in layout:
        second.append([ref if part is None else ref.at[part] for ref, part in zip(refs, parts)])
        refs = refs[len(parts):]
    if add:
        base, refs = refs[:n_second // 2], refs[n_second // 2:]
    outs, refs = refs[:n_second // 2], refs[n_second // 2:]
    a_f32, b_f32, left, right, a_sem, b_sem = refs
    depth = slots * 3 * HALF
    for s in range(slots):
        for b in range(n_bufs):
            @pl.when(table[2 * s] == b)
            def _():
                pltpu.make_async_copy(bufs[b], a_f32.at[s], a_sem.at[s]).start()
        for n in range(n_second):
            for i in range(len(second[n])):
                @pl.when(table[2 * s + 1] == i)
                def _():
                    pltpu.make_async_copy(second[n][i], b_f32.at[n, s], b_sem.at[n, s]).start()
    for s in range(slots):
        pltpu.make_async_copy(a_f32.at[s], a_f32.at[s], a_sem.at[s]).wait()
        for m in range(2):
            at = (1 - m) * depth + s * 3 * HALF
            for p in range(2):
                hi, lo = split(a_f32[s, m, :, p * HALF:(p + 1) * HALF])
                for i, part in enumerate((hi, lo, hi)):
                    left[p * rows:(p + 1) * rows, at + i * HALF:at + (i + 1) * HALF] = part
        for n in range(n_second):
            pltpu.make_async_copy(b_f32.at[n, s], b_f32.at[n, s], b_sem.at[n, s]).wait()
            at = n % 2 * depth + s * 3 * HALF
            hi, lo = split(b_f32[n, s])
            for i, part in enumerate((hi, hi, lo)):
                right[n // 2, at + i * HALF:at + (i + 1) * HALF, :] = part

    def combine(x, y):
        return x[:, :HALF] - y[:, HALF:], x[:, HALF:] + y[:, :HALF]

    def store(m, side, re_im):
        for p in range(2):
            at = (m, slice(None), slice(p * HALF, (p + 1) * HALF))
            outs[side][at] = re_im[p] + base[side][at] if add else re_im[p]

    for side in range(n_second // 2):
        value = jnp.dot(left[:, depth:], right[side, :depth], preferred_element_type=F32)
        store(0, side, combine(value[:rows], value[rows:]))
        slope = jnp.dot(left[...], right[side], preferred_element_type=F32)
        store(1, side, combine(slope[:rows], slope[rows:]))


def products(bufs, second, table, base=None):
    rows, slots = bufs[0].shape[1], table.shape[0] // 2
    n_second = len(second)
    layout = [[part for _, part in members] for members in second]
    sides = n_second // 2
    operands = [*bufs, *[ref for members in second for ref, _ in members]]
    n_any = len(operands)
    operands += [] if base is None else base
    return pl.pallas_call(
        functools.partial(product_kernel, slots, rows, len(bufs), layout, base is not None),
        out_shape=[jax.ShapeDtypeStruct((2, rows, BLOCK), F32)] * sides,
        grid_spec=pltpu.PrefetchScalarGridSpec(
            num_scalar_prefetch=1,
            grid=(),
            in_specs=[pl.BlockSpec(memory_space=pl.ANY)] * n_any
            + [pl.BlockSpec(memory_space=pltpu.VMEM)] * (len(operands) - n_any),
            out_specs=[pl.BlockSpec(memory_space=pltpu.VMEM)] * sides,
            scratch_shapes=[
                pltpu.VMEM((slots, 2, rows, BLOCK), F32),
                pltpu.VMEM((n_second, slots, HALF, BLOCK), F32),
                pltpu.VMEM((2 * rows, 6 * slots * HALF), BF16),
                pltpu.VMEM((n_second // 2, 6 * slots * HALF, BLOCK), BF16),
                pltpu.SemaphoreType.DMA((slots,)),
                pltpu.SemaphoreType.DMA((n_second, slots)),
            ],
        ),
        compiler_params=pltpu.CompilerParams(vmem_limit_bytes=62 * 2**20),
        cost_estimate=pl.CostEstimate(flops=1024, bytes_accessed=1024, transcendentals=0),
    )(table, *operands)


def after(x, *earlier):
    return lax.optimization_barrier((x, *earlier))[0]


def shards(pairs):
    own = pairs[0]
    sec, row, col = (lax.axis_index(name) for name in ("sec", "row", "col"))
    upper, core = sec % 2, col % 2
    position = upper * 4 + col // 2

    def across(x, by):
        return lax.ppermute(x, "row", [(i, (i + by) % 4) for i in range(4)])

    def both(x, pairs, *earlier):
        x = tuple(after(part, *earlier) if earlier else part for part in x)
        return ring_permute(x[0], pairs), ring_permute(x[1], mirrored(pairs))

    one = both((own, own), UP[0])
    low, high = own[:, :HALF], own[:, HALF:]
    kept = jnp.where(core == 0, low, high)
    near = jnp.stack([swap_cores(jnp.where(core == 0, high, low)), kept])
    crossed = ring_permute(near, CROSS[0])
    two = both(one, UP[1], *one)
    crossed_late = ring_permute(after(near, *one, crossed), CROSS[1])
    three = both(two, UP[2], *two)
    last = after(jnp.where(position == 1, *one), *two, crossed_late)
    last = ring_permute(last, LAST[0])
    inner = (position == 1) | (position == 2)
    near = jnp.where(upper == 1, near, jnp.where(inner, after(crossed_late, *two), crossed))
    right, left = across(near, 1), across(near, -1)
    four = both(three, UP[3], *three)
    very_last = ring_permute(after(last, *three), LAST[1])
    right, left = after(right, *three), after(left, *three)
    far = across(right[0], 1), across(left[1], -1)
    second = [
        [(near, (side, m)), (left, (side, m)), (far[side], m), (right, (side, m))]
        for side in range(2)
        for m in range(2)
    ]
    up, down = zip(one, two, three, four)
    ring = [own, *up, *down, last, very_last]

    def table_of(slots, bufs, members):
        rows = [
            [
                [(bufs.index(b), members.index((k - r) % 4)) for b, k in slots(EARLY[p], LATE[p], r)]
                for r in range(4)
            ]
            for p in range(N_RING)
        ]
        return jnp.array(rows, jnp.int32).reshape(N_RING, 4, -1)[position, row]

    def ordered(early, r):
        return sorted(early, key=lambda slot: (slot[1] - r) % 4 == 2)

    early_bufs, late_bufs = (0, 1, 2, 3, 5, 6, 7), (4, 8, 9, 10)
    early_ring, late_ring = [ring[i] for i in early_bufs], [ring[i] for i in late_bufs]
    close = [[members[i] for i in (0, 1, 3)] for members in second]
    first = table_of(lambda early, late, r: ordered(early, r)[:2], early_bufs, (0, 1, 3))
    third = table_of(lambda early, late, r: ordered(early, r)[2:], early_bufs, (0, 1, 2, 3))
    final = table_of(lambda early, late, r: late, late_bufs, (0, 1, 2, 3))
    total = products(early_ring, close, first)
    total = products(early_ring, second, third, total)
    total = products(late_ring, second, final, total)
    return (total[1] + swap_cores(total[0]))[None]


def solution(mesh):
    placed = (P("sec", None, "row", "col"),)
    return jax.shard_map(
        shards, mesh=mesh, in_specs=placed, out_specs=P("sec", None, "row", "col"), check_vma=False
    )
```

```python
import functools

import jax
import jax.numpy as jnp
from jax import lax
from jax.experimental import pallas as pl
from jax.experimental.pallas import tpu as pltpu
from jax.sharding import PartitionSpec as P

F32, BF16 = jnp.float32, jnp.bfloat16
N_Y, N_RING, N_CORE = 4, 8, 2
ROWS, BLOCK, HALF = 512, 512, 256

UP = [
    [(0, 1), (1, 2), (2, 3), (3, 4)],
    [(2, 3), (3, 4), (4, 5)],
    [(3, 4), (4, 5), (5, 6)],
    [(5, 6), (6, 7)],
]
LAST = [[(1, 2), (2, 1)], [(2, 3), (1, 0)]]
CROSS = [[(4, 0), (7, 3)], [(5, 1), (6, 2)]]
EARLY = [
    [(0, 0), (5, 1), (6, 2)],
    [(0, 1), (1, 0), (5, 2)],
    [(0, 2), (1, 1), (5, 3)],
    [(0, 3), (1, 2), (2, 1)],
    [(1, 3), (2, 2), (3, 1)],
    [(2, 3), (3, 2), (7, 0)],
    [(3, 3), (6, 0), (7, 1)],
    [(5, 0), (6, 1), (7, 2)],
]
LATE = [[(10, 3)], [(9, 3)], [(9, 0)], [(10, 0)], [(8, 0)], [(8, 1)], [(4, 2)], [(4, 3)]]


def ring_permute(x, pairs):
    full = [
        ((2 * y + a // 4) * 8 + (a % 4) * 2 + c, (2 * y + b // 4) * 8 + (b % 4) * 2 + c)
        for y in range(N_Y)
        for a, b in pairs
        for c in range(N_CORE)
    ]
    return lax.ppermute(x, ("sec", "col"), full)


def mirrored(pairs):
    return [((3 - a) % 8, (3 - b) % 8) for a, b in pairs]


def swap_cores(x):
    return lax.ppermute(x, "col", [(i, i ^ 1) for i in range(8)])


def split(x):
    hi = x.astype(BF16)
    return hi, (x - hi.astype(F32)).astype(BF16)


def product_kernel(slots, rows, n_bufs, layout, add, table, *refs):
    bufs, refs = refs[:n_bufs], refs[n_bufs:]
    n_second = len(layout)
    second = []
    for parts in layout:
        second.append([ref if part is None else ref.at[part] for ref, part in zip(refs, parts)])
        refs = refs[len(parts):]
    if add:
        base, refs = refs[:n_second // 2], refs[n_second // 2:]
    outs, refs = refs[:n_second // 2], refs[n_second // 2:]
    a_f32, b_f32, left, right, a_sem, b_sem = refs
    depth = slots * 3 * HALF
    for s in range(slots):
        for b in range(n_bufs):
            @pl.when(table[2 * s] == b)
            def _():
                pltpu.make_async_copy(bufs[b], a_f32.at[s], a_sem.at[s]).start()
        for n in range(n_second):
            for i in range(len(second[n])):
                @pl.when(table[2 * s + 1] == i)
                def _():
                    pltpu.make_async_copy(second[n][i], b_f32.at[n, s], b_sem.at[n, s]).start()
    for s in range(slots):
        pltpu.make_async_copy(a_f32.at[s], a_f32.at[s], a_sem.at[s]).wait()
        for m in range(2):
            at = (1 - m) * depth + s * 3 * HALF
            for p in range(2):
                hi, lo = split(a_f32[s, m, :, p * HALF:(p + 1) * HALF])
                for i, part in enumerate((hi, lo, hi)):
                    left[p * rows:(p + 1) * rows, at + i * HALF:at + (i + 1) * HALF] = part
        for n in range(n_second):
            pltpu.make_async_copy(b_f32.at[n, s], b_f32.at[n, s], b_sem.at[n, s]).wait()
            at = n % 2 * depth + s * 3 * HALF
            hi, lo = split(b_f32[n, s])
            for i, part in enumerate((hi, hi, lo)):
                right[n // 2, at + i * HALF:at + (i + 1) * HALF, :] = part

    def combine(x, y):
        return x[:, :HALF] - y[:, HALF:], x[:, HALF:] + y[:, :HALF]

    def store(m, side, re_im):
        for p in range(2):
            at = (m, slice(None), slice(p * HALF, (p + 1) * HALF))
            outs[side][at] = re_im[p] + base[side][at] if add else re_im[p]

    for side in range(n_second // 2):
        value = jnp.dot(left[:, depth:], right[side, :depth], preferred_element_type=F32)
        store(0, side, combine(value[:rows], value[rows:]))
        slope = jnp.dot(left[...], right[side], preferred_element_type=F32)
        store(1, side, combine(slope[:rows], slope[rows:]))


def products(bufs, second, table, base=None):
    rows, slots = bufs[0].shape[1], table.shape[0] // 2
    n_second = len(second)
    layout = [[part for _, part in members] for members in second]
    sides = n_second // 2
    operands = [*bufs, *[ref for members in second for ref, _ in members]]
    n_any = len(operands)
    operands += [] if base is None else base
    return pl.pallas_call(
        functools.partial(product_kernel, slots, rows, len(bufs), layout, base is not None),
        out_shape=[jax.ShapeDtypeStruct((2, rows, BLOCK), F32)] * sides,
        grid_spec=pltpu.PrefetchScalarGridSpec(
            num_scalar_prefetch=1,
            grid=(),
            in_specs=[pl.BlockSpec(memory_space=pl.ANY)] * n_any
            + [pl.BlockSpec(memory_space=pltpu.VMEM)] * (len(operands) - n_any),
            out_specs=[pl.BlockSpec(memory_space=pltpu.VMEM)] * sides,
            scratch_shapes=[
                pltpu.VMEM((slots, 2, rows, BLOCK), F32),
                pltpu.VMEM((n_second, slots, HALF, BLOCK), F32),
                pltpu.VMEM((2 * rows, 6 * slots * HALF), BF16),
                pltpu.VMEM((n_second // 2, 6 * slots * HALF, BLOCK), BF16),
                pltpu.SemaphoreType.DMA((slots,)),
                pltpu.SemaphoreType.DMA((n_second, slots)),
            ],
        ),
        compiler_params=pltpu.CompilerParams(vmem_limit_bytes=62 * 2**20),
        cost_estimate=pl.CostEstimate(flops=1024, bytes_accessed=1024, transcendentals=0),
    )(table, *operands)


def after(x, *earlier):
    return lax.optimization_barrier((x, *earlier))[0]


def shards(pairs):
    own = pairs[0]
    sec, row, col = (lax.axis_index(name) for name in ("sec", "row", "col"))
    upper, core = sec % 2, col % 2
    position = upper * 4 + col // 2

    def across(x, by):
        return lax.ppermute(x, "row", [(i, (i + by) % 4) for i in range(4)])

    def halves(x):
        low, high = x[:, :HALF], x[:, HALF:]
        return jnp.stack([swap_cores(jnp.where(core == 0, high, low)), jnp.where(core == 0, low, high)])

    def both(x, pairs, *earlier):
        x = tuple(after(part, *earlier) if earlier else part for part in x)
        return ring_permute(x[0], pairs), ring_permute(x[1], mirrored(pairs))

    one = both((own, own), UP[0])
    crossed = ring_permute(own, CROSS[0])
    source = halves(own)
    two = both(one, UP[1], *one)
    crossed_late = ring_permute(after(source, *one, crossed), CROSS[1])
    three = both(two, UP[2], *two)
    last = after(jnp.where(position == 1, *one), *two, crossed_late)
    last = ring_permute(last, LAST[0])
    inner = (position == 1) | (position == 2)
    crossed = halves(crossed)
    near = jnp.where(upper == 1, source, jnp.where(inner, after(crossed_late, *two), crossed))
    right, left = across(near, 1), across(near, -1)
    four = both(three, UP[3], *three)
    very_last = ring_permute(after(last, *three), LAST[1])
    right, left = after(right, *three), after(left, *three)
    far = across(right[0], 1), across(left[1], -1)
    second = [
        [(near, (side, m)), (left, (side, m)), (far[side], m), (right, (side, m))]
        for side in range(2)
        for m in range(2)
    ]
    up, down = zip(one, two, three, four)
    ring = [own, *up, *down, last, very_last]

    def table_of(slots, bufs, members):
        rows = [
            [
                [(bufs.index(b), members.index((k - r) % 4)) for b, k in slots(EARLY[p], LATE[p], r)]
                for r in range(4)
            ]
            for p in range(N_RING)
        ]
        return jnp.array(rows, jnp.int32).reshape(N_RING, 4, -1)[position, row]

    def ordered(early, r):
        return sorted(early, key=lambda slot: (slot[1] - r) % 4 == 2)

    early_bufs, late_bufs = (0, 1, 2, 3, 5, 6, 7), (4, 8, 9, 10)
    early_ring, late_ring = [ring[i] for i in early_bufs], [ring[i] for i in late_bufs]
    close = [[members[i] for i in (0, 1, 3)] for members in second]
    first = table_of(lambda early, late, r: ordered(early, r)[:2], early_bufs, (0, 1, 3))
    third = table_of(lambda early, late, r: ordered(early, r)[2:], early_bufs, (0, 1, 2, 3))
    final = table_of(lambda early, late, r: late, late_bufs, (0, 1, 2, 3))
    total = products(early_ring, close, first)
    total = products(early_ring, second, third, total)
    sent = swap_cores(total[0])
    added = products(late_ring, second, final)
    return (total[1] + sent + added[1] + swap_cores(added[0]))[None]


def solution(mesh):
    placed = (P("sec", None, "row", "col"),)
    return jax.shard_map(
        shards, mesh=mesh, in_specs=placed, out_specs=P("sec", None, "row", "col"), check_vma=False
    )
```
